32 devices in a mesh: expert: 8 (over y, x, core), dp: 4 (over z).
Axes of the slice: x: 2, y: 2, z: 4, core: 2. Of those that a mesh axis runs over, the one named last changes fastest.
Arguments:
- heatmap: bfloat16 [4, 64, 56, 256], P('dp', 'expert'), may hold values from -6 to 6
- labels: int32 [4, 56], P('dp', 'expert'), may hold values from 0 to 7, as said below
- w_in: bfloat16 [8, 2304, 1024], P('expert'), may hold values from -0.125 to 0.125
- w_out: bfloat16 [8, 1024, 256], P('expert'), may hold values from -0.1875 to 0.1875
- b_in: float32 [8, 1024], P('expert'), may hold values from -3 to 3
- cotangent: bfloat16 [4, 64, 56, 256], P('dp', 'expert'), may hold values from -0.29882812 to 0.29882812
Outputs:
- output: bfloat16 [4, 64, 56, 256], P('dp', 'expert')
- grad_w_in: float32 [8, 2304, 1024], P('expert', None, 'dp')
- grad_w_out: float32 [8, 1024, 256], P('expert', 'dp')
- grad_b_in: float32 [8, 1024], P('expert', 'dp')
The draws below stay inside these ranges and needn't reach their ends.
Inputs may be any that keep to these rules, and one draw needn't show every extreme that they name: `labels`: of the tiles of one image, at most 10 carry one label, and some label of the draw is carried by exactly 10; of the 7 tiles of one tile row, at most 2 carry one label, a bound that is reached.
All inputs are finite; a program needn't handle non-finite values.
Results may differ from the reference program's by a relative error of at most 0.0055.
Values may be sent and summed in bfloat16 or wider, within the bound.
A program may use at most 128 MiB of HBM per device.

```python
import jax
import jax.numpy as jnp
from jax import lax

C = 256
HID = 1024
EXPERTS = 8
TILES_DEV = 7
IMAGES = 4
ECAP = 10
N_EXPERT = 8


def draw_labels(key, part):

    def one_image(image_key):
        keys = jax.random.split(image_key, 5)
        hottest = jax.random.randint(keys[0], (), 0, EXPERTS)
        source_rank = jax.random.permutation(keys[1], EXPERTS)
        hot_count = jnp.where(source_rank < ECAP // 2, 2, 0)
        others = jax.random.permutation(keys[2], EXPERTS - 1)
        offset = jax.random.randint(keys[3], (), 0, EXPERTS - 1)
        source = jnp.arange(EXPERTS, dtype=jnp.int32)[:, None]
        position = jnp.arange(TILES_DEV, dtype=jnp.int32)[None, :]
        shifted = position - hot_count[:, None]
        cyclic = (offset + source + shifted) % (EXPERTS - 1)
        other_label = (hottest + 1 + others[cyclic]) % EXPERTS
        chosen = jnp.where(position < hot_count[:, None], hottest, other_label)
        shuffle_keys = jax.random.split(keys[4], EXPERTS)
        orders = jax.vmap(lambda shuffle_key: jax.random.permutation(shuffle_key, TILES_DEV))(shuffle_keys)
        chosen = jnp.take_along_axis(chosen, orders, axis=1)
        return chosen.reshape(-1).astype(jnp.int32)
    return jax.vmap(one_image)(jax.random.split(key, IMAGES))


def shard_levels(own_key, shape, cuts, least, largest):
    loudness = 1.0
    for dim, parts in cuts:
        steps = jax.random.uniform(jax.random.fold_in(jax.random.fold_in(own_key, 6), dim), (parts,), jnp.float32, least / len(cuts), largest / len(cuts))
        loudness = loudness * jnp.repeat(jnp.exp(steps), shape[dim] // parts).reshape((-1,) + (1,) * (len(shape) - 1 - dim))
    return loudness


def centred(stream_key, dims, scale, reach, cuts=(), held_as=jnp.bfloat16):
    level = shard_levels(stream_key, dims, cuts, -0.22, 0.18) if cuts else 1.0
    values = jax.random.normal(stream_key, dims, jnp.float32) * scale * level
    return jnp.minimum(jnp.maximum(values, -reach), reach).astype(held_as)


def setup_inputs(seed: int = 0) -> dict:
    streams_of = jax.random.split(jax.random.key(seed), 7)
    return {
        "heatmap": centred(streams_of[0], (IMAGES, 8 * N_EXPERT, 8 * TILES_DEV, C), 1.0, 6.0, ((0, 4), (1, 8))),
        "labels": draw_labels(jax.random.fold_in(streams_of[6], 71), 0),
        "w_in": centred(streams_of[2], (EXPERTS, 9 * C, HID), (9 * C) ** -0.5, 0.125, ((0, 8),)),
        "w_out": centred(streams_of[3], (EXPERTS, HID, C), HID ** -0.5, 0.1875, ((0, 8),)),
        "b_in": centred(streams_of[4], (EXPERTS, HID), 0.5, 3.0, ((0, 8),), jnp.float32),
        "cotangent": centred(streams_of[5], (IMAGES, 8 * N_EXPERT, 8 * TILES_DEV, C), 0.05, 0.29882812, ((0, 4), (1, 8))),
    }


def gelu_parts(preact):
    normal_cdf = 0.5 * (1.0 + lax.erf(preact * 0.7071067811865476))
    density = jnp.exp(-0.5 * preact * preact) * 0.3989422804014327
    return preact * normal_cdf, normal_cdf + preact * density


def unfold(framed):
    count_tiles = framed.shape[0]
    channels = framed.shape[3]
    windows = []
    for row_shift in range(3):
        for col_shift in range(3):
            windows.append(framed[:, row_shift:row_shift + 8, col_shift:col_shift + 8, :])
    joined = jnp.concatenate(windows, axis=3)
    return joined.reshape(count_tiles * 64, 9 * channels)


def reference(heatmap, labels, w_in, w_out, b_in, cotangent):
    images, rows_all, columns, channels = heatmap.shape
    across = columns // 8
    tiles_image = labels.shape[1]
    hidden_size = w_in.shape[2]
    padded = jnp.pad(heatmap, ((0, 0), (1, 1), (1, 1), (0, 0)))
    flat_labels = labels.reshape(-1)

    def visit(carry, number):
        grad_first, grad_second, grad_bias = carry
        image = number // tiles_image
        within = number % tiles_image
        row_at = (within // across) * 8
        col_at = (within % across) * 8
        anchor = jnp.zeros((), jnp.int32)
        framed = lax.dynamic_slice(padded, (image, row_at, col_at, anchor), (1, 10, 10, channels))
        target = lax.dynamic_slice(cotangent, (image, row_at, col_at, anchor), (1, 8, 8, channels)).reshape(64, channels)
        expert = flat_labels[number]
        patches = unfold(framed)
        preact = jnp.dot(patches, w_in[expert], preferred_element_type=jnp.float32) + b_in[expert]
        activation, gelu_slope = gelu_parts(preact)
        hidden = activation.astype(jnp.bfloat16)
        result = jnp.dot(hidden, w_out[expert], preferred_element_type=jnp.float32).astype(jnp.bfloat16)
        second_term = jnp.dot(hidden.T, target, preferred_element_type=jnp.float32)
        hidden_grad = (jnp.dot(target, w_out[expert].T, preferred_element_type=jnp.float32) * gelu_slope).astype(jnp.bfloat16)
        bias_term = jnp.sum(hidden_grad.astype(jnp.float32), axis=0)
        first_term = jnp.dot(patches.T, hidden_grad, preferred_element_type=jnp.float32)
        carry = (grad_first.at[expert].add(first_term), grad_second.at[expert].add(second_term), grad_bias.at[expert].add(bias_term))
        return carry, result.reshape(8, 8, channels)

    experts = w_in.shape[0]
    start = (jnp.zeros((experts, 9 * channels, hidden_size), jnp.float32), jnp.zeros((experts, hidden_size, channels), jnp.float32), jnp.zeros((experts, hidden_size), jnp.float32))
    numbers = jnp.arange(images * tiles_image, dtype=jnp.int32)
    (grad_first, grad_second, grad_bias), pieces = lax.scan(visit, start, numbers)
    output = pieces.reshape(images, rows_all // 8, across, 8, 8, channels).transpose(0, 1, 3, 2, 4, 5).reshape(heatmap.shape)
    return (output, grad_first, grad_second, grad_bias)
```

```python
import jax
import jax.numpy as jnp
from jax import lax
from jax.sharding import PartitionSpec as P

CAP = 2


def extended(cells, sides, width):
    for axis, dim in sides:
        count = lax.axis_size(axis)
        ends = count - 1
        head = lax.slice_in_dim(cells, 0, width, axis=dim)
        tail = lax.slice_in_dim(cells, cells.shape[dim] - width, cells.shape[dim], axis=dim)
        cells = jnp.concatenate(
            [
                lax.ppermute(tail, axis, [(i, (i + 1) % count) for i in range(ends)]),
                cells,
                lax.ppermute(head, axis, [((i + 1) % count, i) for i in range(ends)]),
            ],
            axis=dim,
        )
    return cells


def gelu_parts(preact):
    normal_cdf = 0.5 * (1.0 + lax.erf(preact * 0.7071067811865476))
    density = jnp.exp(-0.5 * preact * preact) * 0.3989422804014327
    return (preact * normal_cdf, normal_cdf + preact * density)


def unfold(framed):
    count_tiles = framed.shape[0]
    channels = framed.shape[3]
    windows = []
    for row_shift in range(3):
        for col_shift in range(3):
            windows.append(framed[:, row_shift : row_shift + 8, col_shift : col_shift + 8, :])
    joined = jnp.concatenate(windows, axis=3)
    return joined.reshape(count_tiles * 64, 9 * channels)


def contract_rows(left_side, right_side):
    return lax.dot_general(
        left_side, right_side, (((0,), (0,)), ((), ())), preferred_element_type=jnp.float32
    )


def shards(heatmap, labels, w_in, w_out, b_in, cotangent):
    channels = heatmap.shape[3]
    columns = heatmap.shape[2]
    tile_count = columns // 8
    owners = lax.axis_size("expert")
    slot_total = owners * CAP
    capacity = 3 * tile_count // 2
    bordered = extended(heatmap[0], (("expert", 0),), 1)
    bordered = jnp.pad(bordered, ((0, 0), (1, 7), (0, 0)))
    left_part = bordered[:, :columns].reshape(10, tile_count, 8, channels)
    right_part = bordered[:, 8 : columns + 8].reshape(10, tile_count, 8, channels)[:, :, :2]
    framed = (
        jnp.concatenate([left_part, right_part], axis=2)
        .transpose(1, 0, 2, 3)
        .reshape(tile_count, 100 * channels)
    )
    labels_here = labels[0]
    tile_ids = jnp.arange(tile_count, dtype=jnp.int32)
    earlier = (labels_here[None, :] == labels_here[:, None]) & (
        tile_ids[None, :] < tile_ids[:, None]
    )
    order_rank = jnp.sum(earlier.astype(jnp.int32), axis=1)
    slot_index = labels_here * CAP + order_rank
    send_map = (slot_index[None, :] == jnp.arange(slot_total, dtype=jnp.int32)[:, None]).astype(
        jnp.bfloat16
    )
    occupied = jnp.sum(send_map, axis=1).reshape(owners, CAP)
    outgoing = (
        jnp.dot(send_map, framed, preferred_element_type=jnp.float32)
        .astype(jnp.bfloat16)
        .reshape(owners, CAP, 100 * channels)
    )
    target_tiles = (
        cotangent[0]
        .reshape(8, tile_count, 8, channels)
        .transpose(1, 0, 2, 3)
        .reshape(tile_count, 64 * channels)
    )
    target_out = (
        jnp.dot(send_map, target_tiles, preferred_element_type=jnp.float32)
        .astype(jnp.bfloat16)
        .reshape(owners, CAP, 64 * channels)
    )
    occupied_in = lax.all_to_all(occupied, "expert", split_axis=0, concat_axis=0, tiled=True)
    arrived = lax.all_to_all(outgoing, "expert", split_axis=0, concat_axis=0, tiled=True)
    target_in = lax.all_to_all(target_out, "expert", split_axis=0, concat_axis=0, tiled=True)
    live_slots = occupied_in.reshape(slot_total).astype(jnp.float32)
    slot_ids = jnp.arange(slot_total, dtype=jnp.int32)
    position = jnp.sum(
        jnp.where(slot_ids[None, :] < slot_ids[:, None], live_slots[None, :], 0.0), axis=1
    )
    take_map = (
        (position[None, :] == jnp.arange(capacity, dtype=jnp.float32)[:, None])
        & (live_slots[None, :] > 0.5)
    ).astype(jnp.bfloat16)
    compact = jnp.dot(
        take_map, arrived.reshape(slot_total, 100 * channels), preferred_element_type=jnp.float32
    ).astype(jnp.bfloat16)
    target_rows = jnp.dot(
        take_map, target_in.reshape(slot_total, 64 * channels), preferred_element_type=jnp.float32
    ).astype(jnp.bfloat16)
    packed = jnp.concatenate(
        [
            compact.reshape(capacity * 100, channels),
            target_rows.reshape(capacity * 64, channels),
        ],
        axis=0,
    )
    gathered = lax.all_gather(packed, "dp", axis=0, tiled=False)
    images = gathered.shape[0]
    compact = compact.reshape(capacity, 10, 10, channels)
    patches = unfold(compact)
    preact = jnp.dot(patches, w_in[0], preferred_element_type=jnp.float32) + b_in[0]
    hidden = gelu_parts(preact)[0].astype(jnp.bfloat16)
    result = (
        jnp.dot(hidden, w_out[0], preferred_element_type=jnp.float32)
        .astype(jnp.bfloat16)
        .reshape(capacity, 64 * channels)
    )
    result_slots = (
        contract_rows(take_map, result).astype(jnp.bfloat16).reshape(owners, CAP, 64 * channels)
    )
    returned = lax.all_to_all(result_slots, "expert", split_axis=0, concat_axis=0, tiled=True)
    mine = contract_rows(send_map, returned.reshape(slot_total, 64 * channels)).astype(jnp.bfloat16)
    output = (
        mine.reshape(tile_count, 8, 8, channels)
        .transpose(1, 0, 2, 3)
        .reshape(1, 8, columns, channels)
    )
    part = w_in.shape[2] // images
    start = lax.axis_index("dp") * part
    w_first = lax.dynamic_slice_in_dim(w_in[0], start, part, axis=1)
    w_second = lax.dynamic_slice_in_dim(w_out[0], start, part, axis=0)
    bias = lax.dynamic_slice_in_dim(b_in[0], start, part, axis=0)
    all_patches = unfold(
        gathered[:, : capacity * 100].reshape(images * capacity, 10, 10, channels)
    )
    all_targets = gathered[:, capacity * 100 :].reshape(images * capacity * 64, channels)
    preact = jnp.dot(all_patches, w_first, preferred_element_type=jnp.float32) + bias
    activation, gelu_slope = gelu_parts(preact)
    hidden = activation.astype(jnp.bfloat16)
    back_hidden = lax.dot_general(
        all_targets, w_second, (((1,), (1,)), ((), ())), preferred_element_type=jnp.float32
    )
    hidden_grad = (back_hidden * gelu_slope).astype(jnp.bfloat16)
    grad_second = contract_rows(hidden, all_targets)
    grad_bias = jnp.sum(hidden_grad, axis=0, dtype=jnp.float32)
    grad_first = contract_rows(all_patches, hidden_grad)
    return (output, grad_first[None], grad_second[None], grad_bias[None])


def solution(mesh):
    return jax.shard_map(
        shards,
        mesh=mesh,
        in_specs=(
            P("dp", "expert", None, None),
            P("dp", "expert"),
            P("expert", None, None),
            P("expert", None, None),
            P("expert", None),
            P("dp", "expert", None, None),
        ),
        out_specs=(
            P("dp", "expert", None, None),
            P("expert", None, "dp"),
            P("expert", "dp", None),
            P("expert", "dp"),
        ),
        check_vma=False,
    )
```

```python
import functools

import jax
import jax.numpy as jnp
from jax import lax
from jax.experimental import pallas as pl
from jax.experimental.pallas import tpu as pltpu
from jax.sharding import PartitionSpec as P

CAP = 2
SLOT = 176
FRAME = SLOT - 64
MESH = pl.DeviceIdType.MESH


def extended(cells):
    count = lax.axis_size("expert")
    ends = count - 1
    return jnp.concatenate(
        [
            lax.ppermute(cells[-1:], "expert", [(i, i + 1) for i in range(ends)]),
            cells,
            lax.ppermute(cells[:1], "expert", [(i + 1, i) for i in range(ends)]),
        ],
        axis=0,
    )


def gelu_parts(preact):
    normal_cdf = 0.5 * (1.0 + lax.erf(preact * 0.7071067811865476))
    density = jnp.exp(-0.5 * preact * preact) * 0.3989422804014327
    return (preact * normal_cdf, normal_cdf + preact * density)


def contract_rows(left_side, right_side):
    return lax.dot_general(
        left_side, right_side, (((0,), (0,)), ((), ())), preferred_element_type=jnp.float32
    )


def kernel(
    owners,
    images,
    batch,
    send_src,
    take_src,
    back_src,
    mine_src,
    tiles,
    pick,
    w_in,
    w_out,
    b_in,
    out_ref,
    first_ref,
    second_ref,
    bias_ref,
    leaving,
    arrived,
    held,
    patches,
    result,
    going,
    returned,
    send_a,
    recv_a,
    send_b,
    recv_b,
    send_right,
    send_left,
    recv_z,
):
    me = lax.axis_index("expert")
    z = lax.axis_index("dp")
    tile_count = out_ref.shape[0]
    capacity = held.shape[1]
    batches = capacity // batch
    slot_total = owners * CAP
    channels = tiles.shape[2]
    part = w_in.shape[1] // images
    has_right = z < images - 1
    has_left = z > 0

    def peer(step):
        return lax.rem(me + step, owners)

    barrier = pltpu.get_barrier_semaphore()

    @pl.loop(1, owners)
    def _(step):
        pl.semaphore_signal(barrier, inc=1, device_id=(peer(step), z), device_id_type=MESH)

    @pl.when(has_right)
    def _():
        pl.semaphore_signal(barrier, inc=1, device_id=(me, z + 1), device_id_type=MESH)

    @pl.when(has_left)
    def _():
        pl.semaphore_signal(barrier, inc=1, device_id=(me, z - 1), device_id_type=MESH)

    @pl.loop(0, slot_total)
    def _(slot):
        leaving[slot] = tiles[send_src[slot]]

    arrived[slot_total] = jnp.zeros_like(arrived[slot_total])
    first_ref[...] = jnp.zeros_like(first_ref)
    second_ref[...] = jnp.zeros_like(second_ref)
    bias_ref[...] = jnp.zeros_like(bias_ref)
    arrived[pl.ds(me * CAP, CAP)] = leaving[pl.ds(me * CAP, CAP)]

    beside = has_right.astype(jnp.int32) + has_left.astype(jnp.int32)
    pl.semaphore_wait(barrier, owners - 1 + beside)

    def route(source, target, send_sem, recv_sem, to, origin):
        return pltpu.make_async_remote_copy(
            src_ref=source.at[pl.ds(to * CAP, CAP)],
            dst_ref=target.at[pl.ds(origin * CAP, CAP)],
            send_sem=send_sem.at[to],
            recv_sem=recv_sem.at[origin],
            device_id=(to, z),
            device_id_type=MESH,
        )

    @pl.loop(1, owners)
    def _(step):
        route(leaving, arrived, send_a, recv_a, peer(step), me).start()

    @pl.loop(1, owners)
    def _(step):
        other = peer(owners - step)
        route(leaving, arrived, send_a, recv_a, other, other).wait_recv()

    def relay(image, part_at, send_sem, to):
        span = held.at[image, pl.ds(part_at * batch, batch)]
        return pltpu.make_async_remote_copy(
            src_ref=span,
            dst_ref=span,
            send_sem=send_sem.at[image, part_at],
            recv_sem=recv_z.at[image, part_at],
            device_id=(me, to),
            device_id_type=MESH,
        )

    def to_right(image, part_at):
        return relay(image, part_at, send_right, z + 1)

    def to_left(image, part_at):
        return relay(image, part_at, send_left, z - 1)

    @pl.loop(0, batches)
    def _(part_at):
        @pl.loop(0, batch)
        def _(within):
            tile = part_at * batch + within
            held[z, tile] = arrived[take_src[tile]]

        @pl.when(has_right)
        def _():
            to_right(z, part_at).start()

        @pl.when(has_left)
        def _():
            to_left(z, part_at).start()

    def unfold(image, part_at):
        for within in range(batch):
            frame = held[image, part_at * batch + within, 64:SLOT, :]
            for shift in range(9):
                patches[within * 64 : (within + 1) * 64, shift * channels : (shift + 1) * channels] = jnp.dot(
                    pick[shift * 64 : (shift + 1) * 64, :], frame, preferred_element_type=jnp.float32
                ).astype(jnp.bfloat16)

    def columns(block):
        return pl.ds(pl.multiple_of(block * part, part), part)

    def preact_of(block):
        return (
            jnp.dot(patches[...], w_in[:, columns(block)], preferred_element_type=jnp.float32)
            + b_in[pl.ds(block, 1), :]
        )

    def gradients(image, part_at):
        activation, slope = gelu_parts(preact_of(z))
        hidden = activation.astype(jnp.bfloat16)
        target = held[image, pl.ds(part_at * batch, batch), 0:64, :].reshape(batch * 64, channels)
        back = lax.dot_general(
            target,
            w_out[columns(z), :],
            (((1,), (1,)), ((), ())),
            preferred_element_type=jnp.float32,
        )
        hidden_grad = (back * slope).astype(jnp.bfloat16)
        second_ref[...] += contract_rows(hidden, target)
        bias_ref[...] += jnp.sum(hidden_grad.astype(jnp.float32), axis=0, keepdims=True)
        first_ref[...] += contract_rows(hidden_grad, patches[...])

    @pl.loop(0, batches)
    def _(part_at):
        unfold(z, part_at)

        def add(block, total):
            hidden = gelu_parts(preact_of(block))[0].astype(jnp.bfloat16)
            return total + jnp.dot(
                hidden, w_out[columns(block), :], preferred_element_type=jnp.float32
            )

        total = lax.fori_loop(
            0, images, add, jnp.zeros((batch * 64, channels), jnp.float32)
        )
        result[pl.ds(part_at * batch, batch)] = total.astype(jnp.bfloat16).reshape(
            batch, 64, channels
        )

    @pl.loop(0, slot_total)
    def _(slot):
        going[slot] = result[back_src[slot]]

    returned[pl.ds(me * CAP, CAP)] = going[pl.ds(me * CAP, CAP)]

    @pl.loop(1, owners)
    def _(step):
        route(going, returned, send_b, recv_b, peer(step), me).start()

    @pl.loop(0, images * batches)
    def _(index):
        distance = index // batches
        part_at = lax.rem(index, batches)
        low = z - distance
        high = z + distance
        arrives_low = (distance > 0) & (low >= 0)
        arrives_high = (distance > 0) & (high < images)

        @pl.when(arrives_low)
        def _():
            relay(low, part_at, send_right, z).wait_recv()

            @pl.when(has_right)
            def _():
                to_right(low, part_at).start()

        @pl.when(arrives_high)
        def _():
            relay(high, part_at, send_left, z).wait_recv()

            @pl.when(has_left)
            def _():
                to_left(high, part_at).start()

        @pl.loop(0, 2)
        def _(side):
            image = jnp.where(side == 0, low, high)

            @pl.when((image >= 0) & (image < images) & ((distance > 0) | (side == 0)))
            def _():
                unfold(image, part_at)
                gradients(image, part_at)

    @pl.loop(1, owners)
    def _(step):
        other = peer(owners - step)
        route(going, returned, send_b, recv_b, other, other).wait_recv()

    @pl.loop(0, tile_count)
    def _(tile):
        out_ref[tile] = returned[mine_src[tile]]

    @pl.loop(1, owners)
    def _(step):
        other = peer(step)
        route(leaving, arrived, send_a, recv_a, other, me).wait_send()
        route(going, returned, send_b, recv_b, other, me).wait_send()

    @pl.loop(0, images * batches)
    def _(index):
        image = index // batches
        part_at = lax.rem(index, batches)

        @pl.when(has_right & (image <= z))
        def _():
            to_right(image, part_at).wait_send()

        @pl.when(has_left & (image >= z))
        def _():
            to_left(image, part_at).wait_send()


def pick_matrix():
    row = jnp.arange(9 * 64, dtype=jnp.int32)
    shift = row // 64
    cell = row % 64
    wanted = (cell // 8 + shift // 3) * 10 + cell % 8 + shift % 3
    return (wanted[:, None] == jnp.arange(FRAME, dtype=jnp.int32)[None, :]).astype(jnp.bfloat16)


def shards(heatmap, labels, w_in, w_out, b_in, cotangent):
    channels = heatmap.shape[3]
    columns = heatmap.shape[2]
    tile_count = columns // 8
    owners = lax.axis_size("expert")
    images = lax.axis_size("dp")
    slot_total = owners * CAP
    capacity = 3 * tile_count // 2
    batch = max(b for b in range(1, 8) if capacity % b == 0)
    hidden_size = w_in.shape[2]
    part = hidden_size // images
    every = lax.all_gather(labels[0], "expert", axis=0, tiled=False)
    bordered = extended(heatmap[0])
    bordered = jnp.pad(bordered, ((0, 0), (1, 7), (0, 0)))
    left_part = bordered[:, :columns].reshape(10, tile_count, 8, channels)
    right_part = bordered[:, 8 : columns + 8].reshape(10, tile_count, 8, channels)[:, :, :2]
    framed = (
        jnp.concatenate([left_part, right_part], axis=2)
        .transpose(1, 0, 2, 3)
        .reshape(tile_count, 100, channels)
    )
    targets = (
        cotangent[0]
        .reshape(8, tile_count, 8, channels)
        .transpose(1, 0, 2, 3)
        .reshape(tile_count, 64, channels)
    )
    tiles = jnp.concatenate([targets, framed], axis=1)
    tiles = jnp.pad(tiles, ((0, 1), (0, SLOT - 164), (0, 0)))

    labels_here = labels[0]
    tile_ids = jnp.arange(tile_count, dtype=jnp.int32)
    earlier = (labels_here[None, :] == labels_here[:, None]) & (
        tile_ids[None, :] < tile_ids[:, None]
    )
    slot_index = labels_here * CAP + jnp.sum(earlier.astype(jnp.int32), axis=1)
    slot_ids = jnp.arange(slot_total, dtype=jnp.int32)
    send_src = tile_count + jnp.sum(
        jnp.where(
            slot_index[None, :] == slot_ids[:, None], tile_ids[None, :] - tile_count, 0
        ),
        axis=1,
    )
    counts = jnp.sum((every == lax.axis_index("expert")).astype(jnp.int32), axis=1)
    live = (slot_ids % CAP) < jnp.broadcast_to(counts[:, None], (owners, CAP)).reshape(slot_total)
    position = jnp.sum(
        ((slot_ids[None, :] < slot_ids[:, None]) & live[None, :]).astype(jnp.int32), axis=1
    )
    places = jnp.arange(capacity, dtype=jnp.int32)
    take_src = slot_total + jnp.sum(
        jnp.where(
            (position[None, :] == places[:, None]) & live[None, :],
            slot_ids[None, :] - slot_total,
            0,
        ),
        axis=1,
    )
    back_src = jnp.minimum(position, capacity - 1)

    smem = pl.BlockSpec(memory_space=pltpu.SMEM)
    vmem = pl.BlockSpec(memory_space=pltpu.VMEM)
    bf16 = jnp.bfloat16
    dma = pltpu.SemaphoreType.DMA
    batches = capacity // batch
    out, first, second, bias = pl.pallas_call(
        functools.partial(kernel, owners, images, batch),
        out_shape=(
            jax.ShapeDtypeStruct((tile_count, 64, channels), bf16),
            jax.ShapeDtypeStruct((part, 9 * channels), jnp.float32),
            jax.ShapeDtypeStruct((part, channels), jnp.float32),
            jax.ShapeDtypeStruct((1, part), jnp.float32),
        ),
        in_specs=[smem] * 4 + [vmem] * 5,
        out_specs=(vmem,) * 4,
        scratch_shapes=[
            pltpu.VMEM((slot_total, SLOT, channels), bf16),
            pltpu.VMEM((slot_total + 1, SLOT, channels), bf16),
            pltpu.VMEM((images, capacity, SLOT, channels), bf16),
            pltpu.VMEM((batch * 64, 9 * channels), bf16),
            pltpu.VMEM((capacity, 64, channels), bf16),
            pltpu.VMEM((slot_total, 64, channels), bf16),
            pltpu.VMEM((slot_total, 64, channels), bf16),
            dma((owners,)),
            dma((owners,)),
            dma((owners,)),
            dma((owners,)),
            dma((images, batches)),
            dma((images, batches)),
            dma((images, batches)),
        ],
        compiler_params=pltpu.CompilerParams(
            collective_id=0, has_side_effects=True, vmem_limit_bytes=60 * 2**20
        ),
    )(
        send_src,
        take_src,
        back_src,
        slot_index,
        tiles,
        pick_matrix(),
        w_in[0],
        w_out[0],
        b_in[0].reshape(images, part),
    )
    output = (
        out.reshape(tile_count, 8, 8, channels)
        .transpose(1, 0, 2, 3)
        .reshape(1, 8, columns, channels)
    )
    return (output, first.T[None], second[None], bias)


def solution(mesh):
    return jax.shard_map(
        shards,
        mesh=mesh,
        in_specs=(
            P("dp", "expert", None, None),
            P("dp", "expert"),
            P("expert", None, None),
            P("expert", None, None),
            P("expert", None),
            P("dp", "expert", None, None),
        ),
        out_specs=(
            P("dp", "expert", None, None),
            P("expert", None, "dp"),
            P("expert", "dp", None),
            P("expert", "dp"),
        ),
        check_vma=False,
    )
```

```python
import functools

import jax
import jax.numpy as jnp
from jax import lax
from jax.experimental import pallas as pl
from jax.experimental.pallas import tpu as pltpu
from jax.sharding import PartitionSpec as P

CAP = 2
FRAME = 112
MESH = pl.DeviceIdType.MESH


def extended(cells):
    count = lax.axis_size("expert")
    ends = count - 1
    return jnp.concatenate(
        [
            lax.ppermute(cells[-1:], "expert", [(i, i + 1) for i in range(ends)]),
            cells,
            lax.ppermute(cells[:1], "expert", [(i + 1, i) for i in range(ends)]),
        ],
        axis=0,
    )


def gelu_parts(preact):
    normal_cdf = 0.5 * (1.0 + lax.erf(preact * 0.7071067811865476))
    density = jnp.exp(-0.5 * preact * preact) * 0.3989422804014327
    return (preact * normal_cdf, normal_cdf + preact * density)


def contract_rows(left_side, right_side):
    return lax.dot_general(
        left_side, right_side, (((0,), (0,)), ((), ())), preferred_element_type=jnp.float32
    )


def kernel(
    owners,
    images,
    batch,
    send_src,
    take_src,
    back_src,
    mine_src,
    targets,
    frames,
    w_in,
    w_out,
    b_in,
    out_ref,
    first_ref,
    second_ref,
    bias_ref,
    leaving_t,
    leaving_f,
    arrived_t,
    arrived_f,
    held_t,
    held_f,
    pick,
    patches,
    result,
    going,
    returned,
    send_t,
    recv_t,
    send_f,
    recv_f,
    send_o,
    recv_o,
    send_right,
    send_left,
    recv_z,
):
    me = lax.axis_index("expert")
    z = lax.axis_index("dp")
    tile_count = out_ref.shape[0]
    capacity = held_t.shape[1]
    batches = capacity // batch
    slot_total = owners * CAP
    channels = targets.shape[2]
    part = w_in.shape[1] // images
    has_right = z < images - 1
    has_left = z > 0

    def peer(step):
        return lax.rem(me + step, owners)

    barrier = pltpu.get_barrier_semaphore()

    @pl.loop(1, owners)
    def _(step):
        pl.semaphore_signal(barrier, inc=1, device_id=(peer(step), z), device_id_type=MESH)

    @pl.when(has_right)
    def _():
        pl.semaphore_signal(barrier, inc=1, device_id=(me, z + 1), device_id_type=MESH)

    @pl.when(has_left)
    def _():
        pl.semaphore_signal(barrier, inc=1, device_id=(me, z - 1), device_id_type=MESH)

    @pl.loop(0, slot_total)
    def _(slot):
        leaving_t[slot] = targets[send_src[slot]]
        leaving_f[slot] = frames[send_src[slot]]

    own_slots = pl.ds(me * CAP, CAP)
    arrived_t[slot_total] = jnp.zeros_like(arrived_t[slot_total])
    arrived_f[slot_total] = jnp.zeros_like(arrived_f[slot_total])
    arrived_t[own_slots] = leaving_t[own_slots]
    arrived_f[own_slots] = leaving_f[own_slots]

    beside = has_right.astype(jnp.int32) + has_left.astype(jnp.int32)
    pl.semaphore_wait(barrier, owners - 1 + beside)

    def route(source, target, send_sem, recv_sem, to, origin):
        return pltpu.make_async_remote_copy(
            src_ref=source.at[pl.ds(to * CAP, CAP)],
            dst_ref=target.at[pl.ds(origin * CAP, CAP)],
            send_sem=send_sem.at[to],
            recv_sem=recv_sem.at[origin],
            device_id=(to, z),
            device_id_type=MESH,
        )

    @pl.loop(1, owners)
    def _(step):
        route(leaving_t, arrived_t, send_t, recv_t, peer(step), me).start()

    @pl.loop(1, owners)
    def _(step):
        route(leaving_f, arrived_f, send_f, recv_f, peer(step), me).start()

    first_ref[...] = jnp.zeros_like(first_ref)
    second_ref[...] = jnp.zeros_like(second_ref)
    bias_ref[...] = jnp.zeros_like(bias_ref)
    cell = lax.broadcasted_iota(jnp.int32, (64, FRAME), 0)
    place = lax.broadcasted_iota(jnp.int32, (64, FRAME), 1)
    for shift in range(9):
        wanted = (cell // 8 + shift // 3) * 10 + cell % 8 + shift % 3
        pick[shift * 64 : (shift + 1) * 64, :] = jnp.where(wanted == place, 1.0, 0.0).astype(
            jnp.bfloat16
        )

    def relay(held, image, first, size, unit, send_sem, to):
        span = held.at[image, pl.ds(first, size)]
        return pltpu.make_async_remote_copy(
            src_ref=span,
            dst_ref=span,
            send_sem=send_sem.at[image, unit],
            recv_sem=recv_z.at[image, unit],
            device_id=(me, to),
            device_id_type=MESH,
        )

    def relay_t(image, send_sem, to):
        return relay(held_t, image, 0, capacity, batches, send_sem, to)

    def relay_f(image, part_at, send_sem, to):
        return relay(held_f, image, part_at * batch, batch, part_at, send_sem, to)

    def on_right(image, make):
        @pl.when(has_right)
        def _():
            make(image, send_right, z + 1).start()

    def on_left(image, make):
        @pl.when(has_left)
        def _():
            make(image, send_left, z - 1).start()

    def on_both(image, make):
        @pl.when(has_right & (image <= z))
        def _():
            make(image, send_right, z + 1)

        @pl.when(has_left & (image >= z))
        def _():
            make(image, send_left, z - 1)

    def wait_all(source, target, send_sem, recv_sem):
        @pl.loop(1, owners)
        def _(step):
            other = peer(owners - step)
            route(source, target, send_sem, recv_sem, other, other).wait_recv()

    wait_all(leaving_t, arrived_t, send_t, recv_t)

    @pl.loop(0, capacity)
    def _(tile):
        held_t[z, tile] = arrived_t[take_src[tile]]

    on_both(z, lambda *where: relay_t(*where).start())
    wait_all(leaving_f, arrived_f, send_f, recv_f)

    @pl.loop(0, batches)
    def _(part_at):
        @pl.loop(0, batch)
        def _(within):
            tile = part_at * batch + within
            held_f[z, tile] = arrived_f[take_src[tile]]

        on_both(z, lambda image, sem, to: relay_f(image, part_at, sem, to).start())

    def unfold(image, part_at):
        for within in range(batch):
            frame = held_f[image, part_at * batch + within]
            for shift in range(9):
                patches[within * 64 : (within + 1) * 64, shift * channels : (shift + 1) * channels] = jnp.dot(
                    pick[shift * 64 : (shift + 1) * 64, :], frame, preferred_element_type=jnp.float32
                ).astype(jnp.bfloat16)

    def columns(block):
        return pl.ds(pl.multiple_of(block * part, part), part)

    def preact_of(block):
        return (
            jnp.dot(patches[...], w_in[:, columns(block)], preferred_element_type=jnp.float32)
            + b_in[:, columns(block)]
        )

    def gradients(image, part_at):
        activation, slope = gelu_parts(preact_of(z))
        hidden = activation.astype(jnp.bfloat16)
        target = held_t[image, pl.ds(part_at * batch, batch)].reshape(batch * 64, channels)
        back = lax.dot_general(
            target,
            w_out[columns(z), :],
            (((1,), (1,)), ((), ())),
            preferred_element_type=jnp.float32,
        )
        hidden_grad = (back * slope).astype(jnp.bfloat16)
        second_ref[...] += contract_rows(hidden, target)
        bias_ref[...] += jnp.sum(hidden_grad.astype(jnp.float32), axis=0, keepdims=True)
        first_ref[...] += contract_rows(hidden_grad, patches[...])

    @pl.loop(0, batches)
    def _(part_at):
        unfold(z, part_at)

        def add(block, total):
            hidden = gelu_parts(preact_of(block))[0].astype(jnp.bfloat16)
            return total + jnp.dot(
                hidden, w_out[columns(block), :], preferred_element_type=jnp.float32
            )

        total = lax.fori_loop(
            0, images, add, jnp.zeros((batch * 64, channels), jnp.float32)
        )
        result[pl.ds(part_at * batch, batch)] = total.astype(jnp.bfloat16).reshape(
            batch, 64, channels
        )

        gradients(z, part_at)

    @pl.loop(0, slot_total)
    def _(slot):
        going[slot] = result[back_src[slot]]

    returned[pl.ds(me * CAP, CAP)] = going[pl.ds(me * CAP, CAP)]

    @pl.loop(1, owners)
    def _(step):
        route(going, returned, send_o, recv_o, peer(step), me).start()

    @pl.loop(1, images)
    def _(distance):
        low = z - distance
        high = z + distance
        arrives_low = low >= 0
        arrives_high = high < images

        @pl.when(arrives_low)
        def _():
            relay_t(low, send_right, z).wait_recv()
            on_right(low, relay_t)

        @pl.when(arrives_high)
        def _():
            relay_t(high, send_left, z).wait_recv()
            on_left(high, relay_t)

        @pl.loop(0, batches)
        def _(part_at):
            def frames_of(image, send_sem, to):
                return relay_f(image, part_at, send_sem, to)

            @pl.when(arrives_low)
            def _():
                frames_of(low, send_right, z).wait_recv()
                on_right(low, frames_of)

            @pl.when(arrives_high)
            def _():
                frames_of(high, send_left, z).wait_recv()
                on_left(high, frames_of)

            @pl.loop(0, 2)
            def _(side):
                image = jnp.where(side == 0, low, high)

                @pl.when((image >= 0) & (image < images))
                def _():
                    unfold(image, part_at)
                    gradients(image, part_at)

    @pl.loop(1, owners)
    def _(step):
        other = peer(owners - step)
        route(going, returned, send_o, recv_o, other, other).wait_recv()

    @pl.loop(0, tile_count)
    def _(tile):
        out_ref[tile] = returned[mine_src[tile]]

    @pl.loop(1, owners)
    def _(step):
        other = peer(step)
        route(leaving_t, arrived_t, send_t, recv_t, other, me).wait_send()
        route(leaving_f, arrived_f, send_f, recv_f, other, me).wait_send()
        route(going, returned, send_o, recv_o, other, me).wait_send()

    @pl.loop(0, images)
    def _(image):
        on_both(image, lambda *where: relay_t(*where).wait_send())

        @pl.loop(0, batches)
        def _(part_at):
            on_both(image, lambda here, sem, to: relay_f(here, part_at, sem, to).wait_send())


def shards(heatmap, labels, w_in, w_out, b_in, cotangent):
    channels = heatmap.shape[3]
    columns = heatmap.shape[2]
    tile_count = columns // 8
    owners = lax.axis_size("expert")
    images = lax.axis_size("dp")
    slot_total = owners * CAP
    capacity = 3 * tile_count // 2
    batch = max(b for b in range(1, 8) if capacity % b == 0)
    hidden_size = w_in.shape[2]
    part = hidden_size // images
    expert_ids = jnp.arange(owners, dtype=jnp.int32)
    wanted = jnp.sum((labels[0][None, :] == expert_ids[:, None]).astype(jnp.int32), axis=1)
    counts = lax.all_to_all(wanted, "expert", split_axis=0, concat_axis=0, tiled=True)
    bordered = extended(heatmap[0])
    bordered = jnp.pad(bordered, ((0, 0), (1, 7), (0, 0)))
    left_part = bordered[:, :columns].reshape(10, tile_count, 8, channels)
    right_part = bordered[:, 8 : columns + 8].reshape(10, tile_count, 8, channels)[:, :, :2]
    framed = (
        jnp.concatenate([left_part, right_part], axis=2)
        .transpose(1, 0, 2, 3)
        .reshape(tile_count, 100, channels)
    )
    targets = (
        cotangent[0]
        .reshape(8, tile_count, 8, channels)
        .transpose(1, 0, 2, 3)
        .reshape(tile_count, 64, channels)
    )
    frames = jnp.pad(framed, ((0, 0), (0, FRAME - 100), (0, 0)))
    labels_here = labels[0]
    tile_ids = jnp.arange(tile_count, dtype=jnp.int32)
    earlier = (labels_here[None, :] == labels_here[:, None]) & (
        tile_ids[None, :] < tile_ids[:, None]
    )
    slot_index = labels_here * CAP + jnp.sum(earlier.astype(jnp.int32), axis=1)
    slot_ids = jnp.arange(slot_total, dtype=jnp.int32)
    send_src = jnp.sum(
        jnp.where(slot_index[None, :] == slot_ids[:, None], tile_ids[None, :], 0), axis=1
    )
    live = (slot_ids % CAP) < jnp.broadcast_to(counts[:, None], (owners, CAP)).reshape(slot_total)
    position = jnp.sum(
        ((slot_ids[None, :] < slot_ids[:, None]) & live[None, :]).astype(jnp.int32), axis=1
    )
    places = jnp.arange(capacity, dtype=jnp.int32)
    take_src = slot_total + jnp.sum(
        jnp.where(
            (position[None, :] == places[:, None]) & live[None, :],
            slot_ids[None, :] - slot_total,
            0,
        ),
        axis=1,
    )
    back_src = jnp.minimum(position, capacity - 1)

    smem = pl.BlockSpec(memory_space=pltpu.SMEM)
    vmem = pl.BlockSpec(memory_space=pltpu.VMEM)
    bf16 = jnp.bfloat16
    dma = pltpu.SemaphoreType.DMA
    batches = capacity // batch
    out, first, second, bias = pl.pallas_call(
        functools.partial(kernel, owners, images, batch),
        out_shape=(
            jax.ShapeDtypeStruct((tile_count, 64, channels), bf16),
            jax.ShapeDtypeStruct((part, 9 * channels), jnp.float32),
            jax.ShapeDtypeStruct((part, channels), jnp.float32),
            jax.ShapeDtypeStruct((1, part), jnp.float32),
        ),
        in_specs=[smem] * 4 + [vmem] * 5,
        out_specs=(vmem,) * 4,
        scratch_shapes=[
            pltpu.VMEM((slot_total, 64, channels), bf16),
            pltpu.VMEM((slot_total, FRAME, channels), bf16),
            pltpu.VMEM((slot_total + 1, 64, channels), bf16),
            pltpu.VMEM((slot_total + 1, FRAME, channels), bf16),
            pltpu.VMEM((images, capacity, 64, channels), bf16),
            pltpu.VMEM((images, capacity, FRAME, channels), bf16),
            pltpu.VMEM((9 * 64, FRAME), bf16),
            pltpu.VMEM((batch * 64, 9 * channels), bf16),
            pltpu.VMEM((capacity, 64, channels), bf16),
            pltpu.VMEM((slot_total, 64, channels), bf16),
            pltpu.VMEM((slot_total, 64, channels), bf16),
        ]
        + [dma((owners,))] * 6
        + [dma((images, batches + 1))] * 3,
        compiler_params=pltpu.CompilerParams(
            collective_id=0, has_side_effects=True, vmem_limit_bytes=60 * 2**20
        ),
    )(
        send_src,
        take_src,
        back_src,
        slot_index,
        targets,
        frames,
        w_in[0],
        w_out[0],
        b_in,
    )
    output = (
        out.reshape(tile_count, 8, 8, channels)
        .transpose(1, 0, 2, 3)
        .reshape(1, 8, columns, channels)
    )
    return (output, first.T[None], second[None], bias)


def solution(mesh):
    return jax.shard_map(
        shards,
        mesh=mesh,
        in_specs=(
            P("dp", "expert", None, None),
            P("dp", "expert"),
            P("expert", None, None),
            P("expert", None, None),
            P("expert", None),
            P("dp", "expert", None, None),
        ),
        out_specs=(
            P("dp", "expert", None, None),
            P("expert", None, "dp"),
            P("expert", "dp", None),
            P("expert", "dp"),
        ),
        check_vma=False,
    )
```

```python
import functools

import jax
import jax.numpy as jnp
from jax import lax
from jax.experimental import pallas as pl
from jax.experimental.pallas import tpu as pltpu
from jax.sharding import PartitionSpec as P

CAP = 2
FRAME = 112
MESH = pl.DeviceIdType.MESH


def extended(cells):
    count = lax.axis_size("expert")
    ends = count - 1
    return jnp.concatenate(
        [
            lax.ppermute(cells[-1:], "expert", [(i, i + 1) for i in range(ends)]),
            cells,
            lax.ppermute(cells[:1], "expert", [(i + 1, i) for i in range(ends)]),
        ],
        axis=0,
    )


def gelu_parts(preact):
    normal_cdf = 0.5 * (1.0 + lax.erf(preact * 0.7071067811865476))
    density = jnp.exp(-0.5 * preact * preact) * 0.3989422804014327
    return (preact * normal_cdf, normal_cdf + preact * density)


def contract_rows(left_side, right_side):
    return lax.dot_general(
        left_side, right_side, (((0,), (0,)), ((), ())), preferred_element_type=jnp.float32
    )


def kernel(
    owners,
    images,
    batch,
    send_src,
    take_src,
    back_src,
    mine_src,
    targets,
    frames,
    w_in,
    w_out,
    b_in,
    out_ref,
    first_ref,
    second_ref,
    bias_ref,
    leaving_t,
    leaving_f,
    arrived_t,
    arrived_f,
    held_t,
    held_f,
    pick,
    patches,
    result,
    going,
    returned,
    send_t,
    recv_t,
    send_f,
    recv_f,
    send_o,
    recv_o,
    send_right,
    send_left,
    recv_z,
):
    me = lax.axis_index("expert")
    z = lax.axis_index("dp")
    tile_count = out_ref.shape[0]
    capacity = held_t.shape[1]
    batches = capacity // batch
    slot_total = owners * CAP
    channels = targets.shape[2]
    part = w_in.shape[1] // images
    has_right = z < images - 1
    has_left = z > 0

    def peer(step):
        return lax.rem(me + step, owners)

    barrier = pltpu.get_barrier_semaphore()

    @pl.loop(1, owners)
    def _(step):
        pl.semaphore_signal(barrier, inc=1, device_id=(peer(step), z), device_id_type=MESH)

    @pl.when(has_right)
    def _():
        pl.semaphore_signal(barrier, inc=1, device_id=(me, z + 1), device_id_type=MESH)

    @pl.when(has_left)
    def _():
        pl.semaphore_signal(barrier, inc=1, device_id=(me, z - 1), device_id_type=MESH)

    @pl.loop(0, slot_total)
    def _(slot):
        leaving_t[slot] = targets[send_src[slot]]
        leaving_f[slot] = frames[send_src[slot]]

    own_slots = pl.ds(me * CAP, CAP)
    arrived_t[slot_total] = jnp.zeros_like(arrived_t[slot_total])
    arrived_f[slot_total] = jnp.zeros_like(arrived_f[slot_total])
    arrived_t[own_slots] = leaving_t[own_slots]
    arrived_f[own_slots] = leaving_f[own_slots]

    beside = has_right.astype(jnp.int32) + has_left.astype(jnp.int32)
    pl.semaphore_wait(barrier, owners - 1 + beside)

    def route(source, target, send_sem, recv_sem, to, origin):
        return pltpu.make_async_remote_copy(
            src_ref=source.at[pl.ds(to * CAP, CAP)],
            dst_ref=target.at[pl.ds(origin * CAP, CAP)],
            send_sem=send_sem.at[to],
            recv_sem=recv_sem.at[origin],
            device_id=(to, z),
            device_id_type=MESH,
        )

    @pl.loop(1, owners)
    def _(step):
        route(leaving_t, arrived_t, send_t, recv_t, peer(step), me).start()

    @pl.loop(1, owners)
    def _(step):
        route(leaving_f, arrived_f, send_f, recv_f, peer(step), me).start()

    first_ref[...] = jnp.zeros_like(first_ref)
    second_ref[...] = jnp.zeros_like(second_ref)
    bias_ref[...] = jnp.zeros_like(bias_ref)
    cell = lax.broadcasted_iota(jnp.int32, (64, FRAME), 0)
    place = lax.broadcasted_iota(jnp.int32, (64, FRAME), 1)
    for shift in range(9):
        wanted = (cell // 8 + shift // 3) * 10 + cell % 8 + shift % 3
        pick[shift * 64 : (shift + 1) * 64, :] = jnp.where(wanted == place, 1.0, 0.0).astype(
            jnp.bfloat16
        )

    def relay(held, image, first, size, unit, send_sem, to):
        span = held.at[image, pl.ds(first, size)]
        return pltpu.make_async_remote_copy(
            src_ref=span,
            dst_ref=span,
            send_sem=send_sem.at[image, unit],
            recv_sem=recv_z.at[image, unit],
            device_id=(me, to),
            device_id_type=MESH,
        )

    def relay_t(image, send_sem, to):
        return relay(held_t, image, 0, capacity, batches, send_sem, to)

    def relay_f(image, part_at, send_sem, to):
        return relay(held_f, image, part_at * batch, batch, part_at, send_sem, to)

    def on_right(image, make):
        @pl.when(has_right)
        def _():
            make(image, send_right, z + 1).start()

    def on_left(image, make):
        @pl.when(has_left)
        def _():
            make(image, send_left, z - 1).start()

    def on_both(image, make):
        @pl.when(has_right & (image <= z))
        def _():
            make(image, send_right, z + 1)

        @pl.when(has_left & (image >= z))
        def _():
            make(image, send_left, z - 1)

    def wait_all(source, target, send_sem, recv_sem):
        @pl.loop(1, owners)
        def _(step):
            other = peer(owners - step)
            route(source, target, send_sem, recv_sem, other, other).wait_recv()

    wait_all(leaving_t, arrived_t, send_t, recv_t)

    @pl.loop(0, capacity)
    def _(tile):
        held_t[z, tile] = arrived_t[take_src[tile]]

    on_both(z, lambda *where: relay_t(*where).start())
    wait_all(leaving_f, arrived_f, send_f, recv_f)

    @pl.loop(0, batches)
    def _(part_at):
        @pl.loop(0, batch)
        def _(within):
            tile = part_at * batch + within
            held_f[z, tile] = arrived_f[take_src[tile]]

        on_both(z, lambda image, sem, to: relay_f(image, part_at, sem, to).start())

    def unfold(image, part_at):
        for within in range(batch):
            frame = held_f[image, part_at * batch + within]
            for shift in range(9):
                patches[within * 64 : (within + 1) * 64, shift * channels : (shift + 1) * channels] = jnp.dot(
                    pick[shift * 64 : (shift + 1) * 64, :], frame, preferred_element_type=jnp.float32
                ).astype(jnp.bfloat16)

    def columns(block):
        return pl.ds(pl.multiple_of(block * part, part), part)

    def preact_of(block):
        return (
            jnp.dot(patches[...], w_in[:, columns(block)], preferred_element_type=jnp.float32)
            + b_in[:, columns(block)]
        )

    def gradients(image, part_at):
        activation, slope = gelu_parts(preact_of(z))
        hidden = activation.astype(jnp.bfloat16)
        target = held_t[image, pl.ds(part_at * batch, batch)].reshape(batch * 64, channels)
        back = lax.dot_general(
            target,
            w_out[columns(z), :],
            (((1,), (1,)), ((), ())),
            preferred_element_type=jnp.float32,
        )
        hidden_grad = (back * slope).astype(jnp.bfloat16)
        second_ref[...] += contract_rows(hidden, target)
        bias_ref[...] += jnp.sum(hidden_grad.astype(jnp.float32), axis=0, keepdims=True)
        first_ref[...] += contract_rows(hidden_grad, patches[...])

    def pass_targets(distance):
        low = z - distance
        high = z + distance

        @pl.when(low >= 0)
        def _():
            relay_t(low, send_right, z).wait_recv()
            on_right(low, relay_t)

        @pl.when(high < images)
        def _():
            relay_t(high, send_left, z).wait_recv()
            on_left(high, relay_t)

    pass_targets(1)

    @pl.loop(0, batches)
    def _(part_at):
        unfold(z, part_at)

        def add(block, total):
            hidden = gelu_parts(preact_of(block))[0].astype(jnp.bfloat16)
            return total + jnp.dot(
                hidden, w_out[columns(block), :], preferred_element_type=jnp.float32
            )

        total = lax.fori_loop(
            0, images, add, jnp.zeros((batch * 64, channels), jnp.float32)
        )
        result[pl.ds(part_at * batch, batch)] = total.astype(jnp.bfloat16).reshape(
            batch, 64, channels
        )

        gradients(z, part_at)

    @pl.loop(0, slot_total)
    def _(slot):
        going[slot] = result[back_src[slot]]

    returned[pl.ds(me * CAP, CAP)] = going[pl.ds(me * CAP, CAP)]

    @pl.loop(1, owners)
    def _(step):
        route(going, returned, send_o, recv_o, peer(step), me).start()

    @pl.loop(1, images)
    def _(distance):
        low = z - distance
        high = z + distance
        arrives_low = low >= 0
        arrives_high = high < images

        @pl.when(distance > 1)
        def _():
            pass_targets(distance)

        @pl.loop(0, batches)
        def _(part_at):
            def frames_of(image, send_sem, to):
                return relay_f(image, part_at, send_sem, to)

            @pl.when(arrives_low)
            def _():
                frames_of(low, send_right, z).wait_recv()
                on_right(low, frames_of)

            @pl.when(arrives_high)
            def _():
                frames_of(high, send_left, z).wait_recv()
                on_left(high, frames_of)

            @pl.loop(0, 2)
            def _(side):
                image = jnp.where(side == 0, low, high)

                @pl.when((image >= 0) & (image < images))
                def _():
                    unfold(image, part_at)
                    gradients(image, part_at)

    @pl.loop(1, owners)
    def _(step):
        other = peer(owners - step)
        route(going, returned, send_o, recv_o, other, other).wait_recv()

    @pl.loop(0, tile_count)
    def _(tile):
        out_ref[tile] = returned[mine_src[tile]]

    @pl.loop(1, owners)
    def _(step):
        other = peer(step)
        route(leaving_t, arrived_t, send_t, recv_t, other, me).wait_send()
        route(leaving_f, arrived_f, send_f, recv_f, other, me).wait_send()
        route(going, returned, send_o, recv_o, other, me).wait_send()

    @pl.loop(0, images)
    def _(image):
        on_both(image, lambda *where: relay_t(*where).wait_send())

        @pl.loop(0, batches)
        def _(part_at):
            on_both(image, lambda here, sem, to: relay_f(here, part_at, sem, to).wait_send())


def shards(heatmap, labels, w_in, w_out, b_in, cotangent):
    channels = heatmap.shape[3]
    columns = heatmap.shape[2]
    tile_count = columns // 8
    owners = lax.axis_size("expert")
    images = lax.axis_size("dp")
    slot_total = owners * CAP
    capacity = 3 * tile_count // 2
    batch = max(b for b in range(1, 8) if capacity % b == 0)
    hidden_size = w_in.shape[2]
    part = hidden_size // images
    expert_ids = jnp.arange(owners, dtype=jnp.int32)
    wanted = jnp.sum((labels[0][None, :] == expert_ids[:, None]).astype(jnp.int32), axis=1)
    counts = lax.all_to_all(wanted, "expert", split_axis=0, concat_axis=0, tiled=True)
    bordered = extended(heatmap[0])
    bordered = jnp.pad(bordered, ((0, 0), (1, 7), (0, 0)))
    left_part = bordered[:, :columns].reshape(10, tile_count, 8, channels)
    right_part = bordered[:, 8 : columns + 8].reshape(10, tile_count, 8, channels)[:, :, :2]
    framed = (
        jnp.concatenate([left_part, right_part], axis=2)
        .transpose(1, 0, 2, 3)
        .reshape(tile_count, 100, channels)
    )
    targets = (
        cotangent[0]
        .reshape(8, tile_count, 8, channels)
        .transpose(1, 0, 2, 3)
        .reshape(tile_count, 64, channels)
    )
    frames = jnp.pad(framed, ((0, 0), (0, FRAME - 100), (0, 0)))
    labels_here = labels[0]
    tile_ids = jnp.arange(tile_count, dtype=jnp.int32)
    earlier = (labels_here[None, :] == labels_here[:, None]) & (
        tile_ids[None, :] < tile_ids[:, None]
    )
    slot_index = labels_here * CAP + jnp.sum(earlier.astype(jnp.int32), axis=1)
    slot_ids = jnp.arange(slot_total, dtype=jnp.int32)
    send_src = jnp.sum(
        jnp.where(slot_index[None, :] == slot_ids[:, None], tile_ids[None, :], 0), axis=1
    )
    live = (slot_ids % CAP) < jnp.broadcast_to(counts[:, None], (owners, CAP)).reshape(slot_total)
    position = jnp.sum(
        ((slot_ids[None, :] < slot_ids[:, None]) & live[None, :]).astype(jnp.int32), axis=1
    )
    places = jnp.arange(capacity, dtype=jnp.int32)
    take_src = slot_total + jnp.sum(
        jnp.where(
            (position[None, :] == places[:, None]) & live[None, :],
            slot_ids[None, :] - slot_total,
            0,
        ),
        axis=1,
    )
    back_src = jnp.minimum(position, capacity - 1)

    smem = pl.BlockSpec(memory_space=pltpu.SMEM)
    vmem = pl.BlockSpec(memory_space=pltpu.VMEM)
    bf16 = jnp.bfloat16
    dma = pltpu.SemaphoreType.DMA
    batches = capacity // batch
    out, first, second, bias = pl.pallas_call(
        functools.partial(kernel, owners, images, batch),
        out_shape=(
            jax.ShapeDtypeStruct((tile_count, 64, channels), bf16),
            jax.ShapeDtypeStruct((part, 9 * channels), jnp.float32),
            jax.ShapeDtypeStruct((part, channels), jnp.float32),
            jax.ShapeDtypeStruct((1, part), jnp.float32),
        ),
        in_specs=[smem] * 4 + [vmem] * 5,
        out_specs=(vmem,) * 4,
        scratch_shapes=[
            pltpu.VMEM((slot_total, 64, channels), bf16),
            pltpu.VMEM((slot_total, FRAME, channels), bf16),
            pltpu.VMEM((slot_total + 1, 64, channels), bf16),
            pltpu.VMEM((slot_total + 1, FRAME, channels), bf16),
            pltpu.VMEM((images, capacity, 64, channels), bf16),
            pltpu.VMEM((images, capacity, FRAME, channels), bf16),
            pltpu.VMEM((9 * 64, FRAME), bf16),
            pltpu.VMEM((batch * 64, 9 * channels), bf16),
            pltpu.VMEM((capacity, 64, channels), bf16),
            pltpu.VMEM((slot_total, 64, channels), bf16),
            pltpu.VMEM((slot_total, 64, channels), bf16),
        ]
        + [dma((owners,))] * 6
        + [dma((images, batches + 1))] * 3,
        compiler_params=pltpu.CompilerParams(
            collective_id=0, has_side_effects=True, vmem_limit_bytes=60 * 2**20
        ),
    )(
        send_src,
        take_src,
        back_src,
        slot_index,
        targets,
        frames,
        w_in[0],
        w_out[0],
        b_in,
    )
    output = (
        out.reshape(tile_count, 8, 8, channels)
        .transpose(1, 0, 2, 3)
        .reshape(1, 8, columns, channels)
    )
    return (output, first.T[None], second[None], bias)


def solution(mesh):
    return jax.shard_map(
        shards,
        mesh=mesh,
        in_specs=(
            P("dp", "expert", None, None),
            P("dp", "expert"),
            P("expert", None, None),
            P("expert", None, None),
            P("expert", None),
            P("dp", "expert", None, None),
        ),
        out_specs=(
            P("dp", "expert", None, None),
            P("expert", None, "dp"),
            P("expert", "dp", None),
            P("expert", "dp"),
        ),
        check_vma=False,
    )
```
